32 devices in a mesh: parts: 2 (over x), tensor: 16 (over z, y, core).
Axes of the slice: x: 2, y: 2, z: 4, core: 2. Of those that a mesh axis runs over, the one named last changes fastest.
Arguments:
- tokens: bfloat16 [128, 6144], P(('parts', 'tensor')), parts along dimension 0, may hold values from -6 to 6
- route_ids: int32 [128, 2], P(('parts', 'tensor')), parts along dimension 0, may hold values from 0 to 3, all different within a row; in each aligned block of 4 rows (0 to 3, 4 to 7, ...) at most 3 rows name the same one
- gate_values: bfloat16 [128, 2], P(('parts', 'tensor')), parts along dimension 0, may hold values from 0.099609375 to 0.8984375
- w_gate: bfloat16 [6144, 32768], P(None, 'tensor'), may hold values from -0.078125 to 0.078125
- w_up: bfloat16 [6144, 32768], P(None, 'tensor'), may hold values from -0.078125 to 0.078125
- w_down: bfloat16 [32768, 6144], P('tensor'), may hold values from -0.0625 to 0.0625
Outputs:
- mixed: bfloat16 [128, 6144], P(('parts', 'tensor')), parts along dimension 0
The draws below stay inside these ranges and needn't reach their ends.
There are 2 independent parts, one for each index of `parts`. The reference program is written for one: setup_inputs(seed, part) draws one part's arguments, and reference() takes and returns one part's arrays. A program takes and returns all parts, laid end to end along the dimension named above; an argument that names none is the same for every part. Nothing has to cross between parts.
Inputs may be any that keep to these rules, and one draw needn't show every extreme that they name: `route_ids`: each row names two different experts; the rows of one device name any one expert at most 3 times, and that bound is reached in every draw.
All inputs are finite; a program needn't handle non-finite values.
Results may differ from the reference program's by a relative error of at most 0.0049.
Values may be sent and summed in bfloat16 or wider, within the bound.
A program may use at most 192 MiB of HBM per device.

```python
import math
import jax
import jax.numpy as jnp
import numpy as np

D = 6144
FF = 8192
EXPERTS = 4
ROWS_DEV = 4
ROWS = 64
MOST = 3


def block_scale(key, shape, shards, least, top_value):
    loudness = 1.0
    for position, blocks in shards:
        steps = jax.random.uniform(jax.random.fold_in(jax.random.fold_in(key, 6), position), (blocks,), jnp.float32, least / len(shards), top_value / len(shards))
        loudness = loudness * jnp.repeat(jnp.exp(steps), shape[position] // blocks).reshape((-1,) + (1,) * (len(shape) - 1 - position))
    return loudness


def shared_out(rng, own, number, rows, number_of, top, reach, slope):
    ranking = jax.random.permutation(rng, number_of)
    crowded, common = shares(number_of, rows * top, reach, slope, True), shares(number_of, rows * top, reach, slope, False)
    places = jnp.arange(number_of)

    def named(lengths, offset_by):
        used = int((lengths > 0).sum())
        fixed = max(1, used // 4)
        shifted = fixed + (places - fixed + offset_by * (used - fixed)) % max(1, number_of - fixed)
        return jnp.zeros((number_of,), jnp.int32).at[ranking[jnp.where(places < fixed, places, shifted)]].set(jnp.asarray(lengths, jnp.int32))

    lengths = jnp.where(number % 4 == 0, named(crowded, number // 4), named(common, number - number // 4 - 1))
    mixed = jax.random.permutation(jax.random.fold_in(own, 3), number_of)
    donor, receiver = mixed[0:number_of // 2 * 2:2], mixed[1:number_of // 2 * 2:2]
    margin = jnp.minimum(lengths[donor] - 1, reach - lengths[receiver]) // 2
    margin = jnp.where((donor == ranking[0]) | (receiver == ranking[0]) | (lengths[receiver] == 0), 0, jnp.maximum(margin, 0))
    shifted = jax.random.randint(jax.random.fold_in(own, 4), (number_of // 2,), 0, 1 << 20) % (margin + 1)
    lengths = lengths.at[donor].add(-shifted).at[receiver].add(shifted)
    labels = jnp.searchsorted(jnp.cumsum(lengths), jnp.arange(rows * top), side="right").astype(jnp.int32)
    grid = labels.reshape(top, rows).T
    grid = grid[jax.random.permutation(jax.random.fold_in(own, 1), rows)]
    offset_by = jax.random.randint(jax.random.fold_in(own, 2), (rows, 1), 0, top)
    return jnp.take_along_axis(grid, (jnp.arange(top)[None, :] + offset_by) % top, axis=1)


def shares(count, total, bound, slope, full):
    weights = [(1 << 20) // math.isqrt(rank ** slope) + 1 for rank in range(1, count + 1)]
    largest = bound if full else min(bound, max(-(-total // count), total * weights[0] // sum(weights)))
    least = 1 if total - largest >= count - 1 else 0
    holding, surplus = [largest] + [least] * (count - 1), total - largest - least * (count - 1)
    while surplus > 0:
        free = [i for i in range(1, count) if holding[i] < largest] or [i for i in range(1, count) if holding[i] < bound]
        whole, remaining = sum([weights[i] for i in free]), surplus
        for i in free:
            extra = min(bound - holding[i], max(1, remaining * weights[i] // whole), surplus)
            holding[i] = holding[i] + extra
            surplus = surplus - extra
    return np.array(holding)


def bell_draw(own_key, extent, spread, limit, cuts=(), held_as=jnp.bfloat16):
    drawn = jax.random.normal(own_key, extent, jnp.float32) * spread
    if len(cuts) > 0:
        drawn = block_scale(own_key, extent, cuts, -0.22, 0.18) * drawn
    return jnp.clip(drawn, min=-limit, max=limit).astype(held_as)


def setup_inputs(seed: int = 0, part: int = 0) -> dict:
    keys = jax.random.split(jax.random.key(seed), 7)
    own_keys = jax.random.split(jax.random.fold_in(keys[6], part), 7)
    tokens = bell_draw(own_keys[0], (ROWS, D), 1.0, 6.0, ((0, 16),))
    route_ids_keys = jax.random.split(jax.random.fold_in(own_keys[1], 1), ROWS // ROWS_DEV)
    route_ids_turns = jax.random.permutation(jax.random.fold_in(own_keys[1], 3), ROWS // ROWS_DEV)
    route_ids = jax.vmap(lambda own, number: shared_out(jax.random.fold_in(own_keys[1], 2), own, number, ROWS_DEV, EXPERTS, 2, MOST, 2))(route_ids_keys, route_ids_turns).reshape((ROWS, 2))
    gate_values = jnp.clip(0.099609375 + 0.7988281 * jax.random.uniform(own_keys[2], (ROWS, 2), jnp.float32) ** block_scale(own_keys[2], (ROWS, 2), ((0, 16),), -0.2, 0.2), 0.099609375, 0.8984375).astype(jnp.bfloat16)
    w_gate = bell_draw(keys[3], (D, EXPERTS * FF), D ** -0.5, 0.078125, ((1, 16),))
    w_up = bell_draw(keys[4], (D, EXPERTS * FF), D ** -0.5, 0.078125, ((1, 16),))
    w_down = bell_draw(keys[5], (EXPERTS * FF, D), FF ** -0.5, 0.0625, ((0, 16),))
    return dict(tokens=tokens, route_ids=route_ids, gate_values=gate_values, w_gate=w_gate, w_up=w_up, w_down=w_down)


def reference(tokens, route_ids, gate_values, w_gate, w_up, w_down):
    total = jnp.zeros((tokens.shape[0], tokens.shape[1]), jnp.float32)
    for expert in range(EXPERTS):
        first = expert * FF
        gate_proj = jnp.dot(tokens, w_gate[:, first:first + FF], preferred_element_type=jnp.float32)
        up_proj = jnp.dot(tokens, w_up[:, first:first + FF], preferred_element_type=jnp.float32)
        hidden = (jax.nn.silu(gate_proj) * up_proj).astype(jnp.bfloat16)
        expert_rows = jnp.dot(hidden, w_down[first:first + FF, :], preferred_element_type=jnp.float32)
        weight = jnp.sum(jnp.where(route_ids == expert, gate_values.astype(jnp.float32), jnp.float32(0.0)), axis=1)
        total = total + weight[:, None] * expert_rows
    return total.astype(jnp.bfloat16)
```

```python
import functools

import jax
import jax.numpy as jnp
from jax import lax
from jax.experimental import pallas as pl
from jax.experimental.pallas import tpu as pltpu
from jax.sharding import PartitionSpec as P

EXPERTS = 4
BLOCK = 128
MOST = 3
DEVICES = 16
ROWS_DEV = 4
FOLD = 4
K_CHUNKS = 8
GU_SLOTS = 4
D_EARLY = 4
CHUNK = 512
SKEW = 2
LANES = 128
MESH = pl.DeviceIdType.MESH


def spread(first, second, upper):
    low = lax.broadcasted_iota(jnp.int32, first.shape, 0) < 4
    if upper:
        return jnp.where(low, pltpu.roll(first, 4, 0), second)
    return jnp.where(low, first, pltpu.roll(second, 4, 0))


def kernel(sizes, tokens, routes, gates, w_gate, w_up, w_down, out, *scratch):
    (block, x, weight, gbuf, ubuf, dbuf, gate_acc, up_acc, hidden,
     send_a, recv_a, keep_a, send_b, recv_b, keep_b, send_c, recv_c, keep_c, folded,
     g_sem, u_sem, d_sem, zs, zr, ys, yr, cs, cr, as_, ar, bs, br, ts, tr) = scratch
    width, hid, chunks = sizes
    quarter = width // FOLD
    k_rows = width // K_CHUNKS
    per_quarter = K_CHUNKS // FOLD
    piece = CHUNK // FOLD
    part = lax.axis_index("parts")
    me = lax.axis_index("tensor")
    z, y, c = me // 4, me // 2 % 2, me % 2

    def index(zz, yy, cc):
        return zz * 4 + yy * 2 + cc

    def z_of(k):
        return (z + k) % 4

    y_peer = index(z, 1 - y, c)
    c_peer = index(z, y, 1 - c)

    def gu_copy(step):
        slot = step % GU_SLOTS
        rows = pl.ds(pl.multiple_of(step * k_rows, k_rows), k_rows)
        return (pltpu.make_async_copy(w_gate.at[rows, :], gbuf.at[slot], g_sem.at[slot]),
                pltpu.make_async_copy(w_up.at[rows, :], ubuf.at[slot], u_sem.at[slot]))

    def d_copy(step):
        columns = pl.ds(pl.multiple_of(step * CHUNK, CHUNK), CHUNK)
        return pltpu.make_async_copy(w_down.at[:, columns], dbuf.at[step], d_sem.at[step])

    for step in range(GU_SLOTS):
        for copy in gu_copy(step):
            copy.start()

    barrier = pltpu.get_barrier_semaphore()
    for peer in [index(z_of(k), y, c) for k in (1, 2, 3)] + [y_peer, c_peer]:
        pl.semaphore_signal(barrier, inc=1, device_id=(part, peer), device_id_type=MESH)

    rows = tokens[...].astype(jnp.float32)
    block[me, :, :quarter] = jnp.concatenate(
        [rows[:, q * quarter:(q + 1) * quarter] for q in range(FOLD)], axis=0
    ).astype(jnp.bfloat16)
    ids = routes[...]
    values = gates[...].astype(jnp.float32)
    weights = []
    for e in range(EXPERTS):
        column = jnp.sum(jnp.where(ids == e, values, 0.0), axis=1, keepdims=True)
        weights.append(jnp.broadcast_to(column, (ROWS_DEV, LANES)))
    block[me, :, quarter:] = jnp.concatenate(weights, axis=0).astype(jnp.bfloat16)

    pl.semaphore_wait(barrier, 5)

    def send(source, target, s_sem, r_sem, peer):
        return pltpu.make_async_remote_copy(
            src_ref=source, dst_ref=target, send_sem=s_sem, recv_sem=r_sem,
            device_id=(part, peer), device_id_type=MESH)

    def z_send(k):
        return send(block.at[me], block.at[me], zs.at[k], zr.at[k], index(z_of(k), y, c))

    def y_send(k):
        own = block.at[index(z_of(4 - k), y, c)]
        return send(own, own, ys.at[k], yr.at[k], y_peer)

    def c_send(dy, k):
        own = block.at[index(z_of(4 - k), (y + dy) % 2, c)]
        return send(own, own, cs.at[dy * 4 + k], cr.at[dy * 4 + k], c_peer)

    def assemble(dy, dc):
        base = dc * 32 + dy * 16
        parts = [block[index(z_of(k), (y + dy) % 2, (c + dc) % 2)].astype(jnp.float32)
                 for k in range(4)]
        chosen = jnp.zeros((16, LANES), jnp.float32)
        for q in range(FOLD):
            tile = slice(q // 2 * 8, q // 2 * 8 + 8)
            pairs = [spread(parts[2 * m][tile], parts[2 * m + 1][tile], q % 2) for m in (0, 1)]
            both = jnp.concatenate(pairs, axis=0)
            for h in range(per_quarter):
                x[q * per_quarter + h, base:base + 16, :] = both[
                    :, h * k_rows:(h + 1) * k_rows].astype(jnp.bfloat16)
            chosen = jnp.where(z == q, both[:, quarter:], chosen)
        weight[base:base + 16, :] = chosen

    for k in (2, 3, 1):
        z_send(k).start()
    y_send(0).start()
    c_send(0, 0).start()
    y_send(0).wait_recv()
    c_send(1, 0).start()
    for k in (1, 3, 2):
        z_send(k).wait_recv()
        y_send(k).start()
        c_send(0, k).start()
    for step in range(min(D_EARLY, chunks)):
        d_copy(step).start()
    gate_acc[...] = jnp.zeros_like(gate_acc)
    up_acc[...] = jnp.zeros_like(up_acc)
    assemble(0, 0)
    for k in (1, 3, 2):
        y_send(k).wait_recv()
        c_send(1, k).start()
    assemble(1, 0)
    for k in range(4):
        c_send(0, k).wait_recv()
    assemble(0, 1)
    for k in range(4):
        c_send(1, k).wait_recv()
    assemble(1, 1)

    tile_n = min(512, hid)

    def gate_up(step, carry):
        slot = step % GU_SLOTS
        lhs = x[step]
        for copy, buffer, total in zip(gu_copy(step), (gbuf, ubuf), (gate_acc, up_acc)):
            copy.wait()
            for n in range(hid // tile_n):
                columns = slice(n * tile_n, (n + 1) * tile_n)
                total[:, columns] += jnp.dot(
                    lhs, buffer[slot, :, columns], preferred_element_type=jnp.float32)

        @pl.when(step + GU_SLOTS < K_CHUNKS)
        def _():
            for copy in gu_copy(step + GU_SLOTS):
                copy.start()

        late = -(-(chunks - D_EARLY) // (K_CHUNKS - GU_SLOTS))
        for i in range(max(late, 0)):
            number = D_EARLY + (step - GU_SLOTS) * late + i

            @pl.when((step >= GU_SLOTS) & (number < chunks))
            def _():
                d_copy(number).start()

        return carry

    lax.fori_loop(0, K_CHUNKS, gate_up, 0)
    for n in range(hid // tile_n):
        columns = slice(n * tile_n, (n + 1) * tile_n)
        gate = gate_acc[:, columns]
        hidden[:, columns] = (gate / (1.0 + jnp.exp(-gate)) * up_acc[:, columns]).astype(jnp.bfloat16)

    def a_send(n):
        return send(send_a.at[n], recv_a.at[n], as_.at[n], ar.at[n], c_peer)

    def b_send(n):
        return send(send_b.at[n], recv_b.at[n], bs.at[n], br.at[n], y_peer)

    def t_send(n, k):
        return send(send_c.at[n, k - 1], recv_c.at[n, k - 1], ts.at[n, k - 1], tr.at[n, k - 1],
                    index(z_of(k), y, c))

    def down(step, carry):
        n_d = step - 3 * SKEW

        @pl.when(n_d >= 0)
        def _():
            for k in (1, 2, 3):
                t_send(n_d, k).wait_recv()
            folded[n_d] = keep_c[n_d] + (
                recv_c[n_d, 0].astype(jnp.float32) + recv_c[n_d, 1].astype(jnp.float32)
                + recv_c[n_d, 2].astype(jnp.float32))

        n_c = step - 2 * SKEW

        @pl.when((n_c >= 0) & (n_c < chunks))
        def _():
            b_send(n_c).wait_recv()
            total = keep_b[n_c] + recv_b[n_c].astype(jnp.float32)
            for k in (2, 1, 3, 0):
                half = total[k // 2 * 8:k // 2 * 8 + 8]
                both = jnp.concatenate(
                    [spread(half[:, 2 * m * piece:(2 * m + 1) * piece],
                            half[:, (2 * m + 1) * piece:(2 * m + 2) * piece], k % 2)
                     for m in (0, 1)], axis=0)
                if k == 0:
                    keep_c[n_c] = both
                else:
                    send_c[n_c, k - 1] = both.astype(jnp.bfloat16)
                    t_send(n_c, k).start()

        n_b = step - SKEW

        @pl.when((n_b >= 0) & (n_b < chunks))
        def _():
            a_send(n_b).wait_recv()
            send_b[n_b] = (keep_a[n_b, 16:, :] + recv_a[n_b, 16:, :].astype(jnp.float32)).astype(jnp.bfloat16)
            b_send(n_b).start()
            keep_b[n_b] = keep_a[n_b, :16, :] + recv_a[n_b, :16, :].astype(jnp.float32)

        @pl.when(step < chunks)
        def _():
            d_copy(step).wait()
            scale = weight[...]
            product = jnp.dot(hidden[...], dbuf[step], preferred_element_type=jnp.float32)
            product = product * jnp.concatenate([scale] * (CHUNK // LANES), axis=1)
            send_a[step] = product[32:].astype(jnp.bfloat16)
            a_send(step).start()
            keep_a[step] = product[:32]

        return carry

    lax.fori_loop(0, chunks + 3 * SKEW, down, 0)

    for n in range(chunks):
        pieces = []
        for j in range(FOLD):
            half = folded[n, j // 2 * 8:j // 2 * 8 + 8, :]
            pieces.append(pltpu.roll(half, 4, 0) if j % 2 else half)
        whole = jnp.concatenate(pieces, axis=1)
        out[:, n * CHUNK:(n + 1) * CHUNK] = whole[:ROWS_DEV].astype(jnp.bfloat16)

    for k in (1, 2, 3):
        z_send(k).wait_send()
    for k in range(4):
        y_send(k).wait_send()
        c_send(0, k).wait_send()
        c_send(1, k).wait_send()

    def drain(n, carry):
        a_send(n).wait_send()
        b_send(n).wait_send()
        for k in (1, 2, 3):
            t_send(n, k).wait_send()
        return carry

    lax.fori_loop(0, chunks, drain, 0)


def fused(tokens, route_ids, gate_values, w_gate, w_up, w_down):
    width = tokens.shape[1]
    hid = w_gate.shape[1]
    chunks = width // CHUNK
    quarter = width // FOLD
    k_rows = width // K_CHUNKS
    piece = CHUNK // FOLD
    rows = DEVICES * ROWS_DEV
    bf16, f32, dma = jnp.bfloat16, jnp.float32, pltpu.SemaphoreType.DMA
    scratch = [
        pltpu.VMEM((DEVICES, 16, quarter + LANES), bf16),
        pltpu.VMEM((K_CHUNKS, rows, k_rows), bf16),
        pltpu.VMEM((rows, LANES), f32),
        pltpu.VMEM((GU_SLOTS, k_rows, hid), bf16),
        pltpu.VMEM((GU_SLOTS, k_rows, hid), bf16),
        pltpu.VMEM((chunks, hid, CHUNK), bf16),
        pltpu.VMEM((rows, hid), f32),
        pltpu.VMEM((rows, hid), f32),
        pltpu.VMEM((rows, hid), bf16),
        pltpu.VMEM((chunks, 32, CHUNK), bf16),
        pltpu.VMEM((chunks, 32, CHUNK), bf16),
        pltpu.VMEM((chunks, 32, CHUNK), f32),
        pltpu.VMEM((chunks, 16, CHUNK), bf16),
        pltpu.VMEM((chunks, 16, CHUNK), bf16),
        pltpu.VMEM((chunks, 16, CHUNK), f32),
        pltpu.VMEM((chunks, 3, 16, piece), bf16),
        pltpu.VMEM((chunks, 3, 16, piece), bf16),
        pltpu.VMEM((chunks, 16, piece), f32),
        pltpu.VMEM((chunks, 16, piece), f32),
        dma((GU_SLOTS,)), dma((GU_SLOTS,)), dma((chunks,)),
        dma((4,)), dma((4,)), dma((4,)), dma((4,)), dma((8,)), dma((8,)),
        dma((chunks,)), dma((chunks,)), dma((chunks,)), dma((chunks,)),
        dma((chunks, 3)), dma((chunks, 3)),
    ]
    vmem = pl.BlockSpec(memory_space=pltpu.VMEM)
    hbm = pl.BlockSpec(memory_space=pl.ANY)
    return pl.pallas_call(
        functools.partial(kernel, (width, hid, chunks)),
        out_shape=jax.ShapeDtypeStruct((ROWS_DEV, width), bf16),
        in_specs=[vmem, vmem, vmem, hbm, hbm, hbm],
        out_specs=vmem,
        scratch_shapes=scratch,
        compiler_params=pltpu.CompilerParams(
            collective_id=0, has_side_effects=True, vmem_limit_bytes=60 * 2**20),
        cost_estimate=pl.CostEstimate(
            flops=6 * rows * width * hid, bytes_accessed=6 * width * hid, transcendentals=rows * hid),
    )(tokens, route_ids, gate_values, w_gate, w_up, w_down)


def partner(shard, axis, stride):
    return lax.ppermute(shard, axis, [(i, i ^ 1 << stride) for i in range(lax.axis_size(axis))])


def from_behind(block, axis, distance):
    devices = range(lax.axis_size(axis))
    route = [((i - distance) % len(devices), i) for i in devices]
    return lax.ppermute(block, axis, route)


def expert_blocks(compact, occupied, w_gate, w_up, w_down):
    capacity = compact.shape[0]

    def block_step(block_index, buffer):

        def block_work(inner):
            block_rows = lax.dynamic_slice_in_dim(compact, block_index * BLOCK, BLOCK, 0)
            gate_proj = jnp.dot(block_rows, w_gate, preferred_element_type=jnp.float32)
            up_proj = jnp.dot(block_rows, w_up, preferred_element_type=jnp.float32)
            hidden = (jax.nn.silu(gate_proj) * up_proj).astype(jnp.bfloat16)
            output_rows = jnp.dot(hidden, w_down, preferred_element_type=jnp.float32)
            return lax.dynamic_update_slice_in_dim(inner, output_rows, block_index * BLOCK, 0)

        def block_skip(inner):
            return inner

        return lax.cond(block_index * BLOCK < occupied, block_work, block_skip, buffer)

    start_buffer = jnp.zeros((capacity, w_down.shape[1]), jnp.float32)
    return lax.fori_loop(0, capacity // BLOCK, block_step, start_buffer)


def per_device(tokens, route_ids, gate_values, w_gate, w_up, w_down):
    tensor_size = lax.axis_size("tensor")
    group_size = tensor_size // EXPERTS
    my_index = lax.axis_index("tensor")
    expert = my_index // group_size
    local_rows = tokens.shape[0]
    width = tokens.shape[1]
    total_rows = local_rows * tensor_size
    capacity = (total_rows + BLOCK - 1) // BLOCK * BLOCK
    all_routes = lax.all_gather(route_ids, "tensor", axis=0, tiled=True)
    routed = all_routes == expert
    selected = jnp.any(routed, axis=1).astype(jnp.int32)
    occupied = jnp.sum(selected)
    expert_list = jnp.arange(EXPERTS, dtype=jnp.int32)
    local_hits = jnp.any(route_ids[:, :, None] == expert_list[None, None, :], axis=1).astype(
        jnp.int32
    )
    local_place = jnp.cumsum(local_hits, axis=0) - 1
    target = jnp.where(local_hits > 0, local_place, MOST)
    row_numbers = jnp.broadcast_to(jnp.arange(local_rows, dtype=jnp.int32)[:, None], target.shape)
    send_rows = (
        jnp.full((EXPERTS, MOST), local_rows, jnp.int32)
        .at[jnp.broadcast_to(expert_list[None, :], target.shape), target]
        .set(row_numbers, mode="drop")
    )
    outgoing = jnp.take(tokens, send_rows.reshape(-1), axis=0, mode="fill", fill_value=0)
    outgoing = outgoing.reshape(EXPERTS, 1, MOST, width)
    outgoing = jnp.broadcast_to(outgoing, (EXPERTS, group_size, MOST, width)).reshape(
        tensor_size * MOST, width
    )
    received = lax.all_to_all(outgoing, "tensor", split_axis=0, concat_axis=0, tiled=True)
    per_source = jnp.sum(selected.reshape(tensor_size, local_rows), axis=1)
    source_start = jnp.cumsum(per_source) - per_source
    place = jnp.arange(MOST, dtype=jnp.int32)
    landing = jnp.where(
        place[None, :] < per_source[:, None], source_start[:, None] + place[None, :], capacity
    )
    inverse = (
        jnp.full((capacity,), tensor_size * MOST, jnp.int32)
        .at[landing.reshape(-1)]
        .set(jnp.arange(tensor_size * MOST, dtype=jnp.int32), mode="drop")
    )
    compact = jnp.take(received, inverse, axis=0, mode="fill", fill_value=0)
    partial_value = expert_blocks(compact, occupied, w_gate, w_up, w_down)
    returning = jnp.take(partial_value, landing.reshape(-1), axis=0, mode="fill", fill_value=0)
    levels = group_size.bit_length() - 1
    buffer = jnp.transpose(returning.reshape(EXPERTS, group_size, MOST, width), (1, 0, 2, 3))
    for bit in range(levels - 1, -1, -1):
        half = buffer.shape[0] // 2
        lower = buffer[:half]
        upper = buffer[half:]
        high_side = my_index >> bit & 1 == 1
        keep = jnp.where(high_side, upper, lower)
        give = jnp.where(high_side, lower, upper)
        buffer = keep + partner(give, "tensor", bit)
    reduced = buffer[0]
    collected = jnp.zeros((EXPERTS, MOST, width), jnp.float32)
    own_piece = lax.dynamic_index_in_dim(reduced, expert, 0, keepdims=True)
    collected = lax.dynamic_update_slice_in_dim(collected, own_piece, expert, 0)
    for offset in range(1, EXPERTS):
        piece = lax.dynamic_index_in_dim(reduced, (expert + offset) % EXPERTS, 0, keepdims=True)
        arrived_piece = from_behind(piece, "tensor", offset * group_size)
        source_expert = (expert - offset + EXPERTS) % EXPERTS
        collected = lax.dynamic_update_slice_in_dim(collected, arrived_piece, source_expert, 0)
    per_expert = collected.reshape(EXPERTS * MOST, width)
    mixed_rows = jnp.zeros((local_rows, width), jnp.float32)
    for column in range(2):
        chosen = route_ids[:, column]
        chosen_place = jnp.take_along_axis(local_place, chosen[:, None], axis=1)[:, 0]
        picked = jnp.take(per_expert, chosen * MOST + chosen_place, axis=0)
        mixed_rows = mixed_rows + gate_values[:, column].astype(jnp.float32)[:, None] * picked
    return mixed_rows.astype(jnp.bfloat16)


def solution(mesh):
    in_specs = (
        P(("parts", "tensor"), None),
        P(("parts", "tensor"), None),
        P(("parts", "tensor"), None),
        P(None, "tensor"),
        P(None, "tensor"),
        P("tensor", None),
    )
    out_specs = P(("parts", "tensor"), None)
    rows = ROWS_DEV * DEVICES

    def whole(tokens, route_ids, gate_values, w_gate, w_up, w_down):
        width, hid = w_gate.shape[0], w_gate.shape[1] // mesh.shape["tensor"]
        fits = mesh.shape["tensor"] == DEVICES and tokens.shape[0] == rows * mesh.shape["parts"]
        fits = fits and width % (K_CHUNKS * LANES) == 0 and hid % 512 == 0
        fits = fits and width * hid <= 6144 * 2048
        return shard(fused if fits else per_device)(
            tokens, route_ids, gate_values, w_gate, w_up, w_down)

    shard = lambda body: jax.shard_map(
        body, mesh=mesh, in_specs=in_specs, out_specs=out_specs, check_vma=False
    )
    return whole
```

```python
import functools

import jax
import jax.numpy as jnp
from jax import lax
from jax.experimental import pallas as pl
from jax.experimental.pallas import tpu as pltpu
from jax.sharding import PartitionSpec as P

EXPERTS = 4
BLOCK = 128
MOST = 3
DEVICES = 16
ROWS_DEV = 4
FOLD = 4
K_CHUNKS = 8
GU_SLOTS = 4
D_EARLY = 8
CHUNK = 512
SKEW = 12
LANES = 128
MESH = pl.DeviceIdType.MESH


def spread(first, second, upper):
    low = lax.broadcasted_iota(jnp.int32, first.shape, 0) < 4
    if upper:
        return jnp.where(low, pltpu.roll(first, 4, 0), second)
    return jnp.where(low, first, pltpu.roll(second, 4, 0))


def kernel(sizes, tokens, by_expert, w_gate, w_up, w_down, out, *scratch):
    (block, x, weight, gbuf, ubuf, dbuf, gate_acc, up_acc, hidden,
     send_a, recv_a, keep_a, send_b, recv_b, keep_b, send_c, recv_c, keep_c, folded,
     g_sem, u_sem, d_sem, zs, zr, ys, yr, cs, cr, as_, ar, bs, br, ts, tr) = scratch
    width, hid, chunks = sizes
    quarter = width // FOLD
    k_rows = width // K_CHUNKS
    per_quarter = K_CHUNKS // FOLD
    piece = CHUNK // FOLD
    part = lax.axis_index("parts")
    me = lax.axis_index("tensor")
    z, y, c = me // 4, me // 2 % 2, me % 2

    def index(zz, yy, cc):
        return zz * 4 + yy * 2 + cc

    def z_of(k):
        return (z + k) % 4

    y_peer = index(z, 1 - y, c)
    c_peer = index(z, y, 1 - c)

    def gu_copy(step):
        slot = step % GU_SLOTS
        rows = pl.ds(pl.multiple_of(step * k_rows, k_rows), k_rows)
        return (pltpu.make_async_copy(w_gate.at[rows, :], gbuf.at[slot], g_sem.at[slot]),
                pltpu.make_async_copy(w_up.at[rows, :], ubuf.at[slot], u_sem.at[slot]))

    def d_copy(step):
        columns = pl.ds(pl.multiple_of(step * CHUNK, CHUNK), CHUNK)
        return pltpu.make_async_copy(w_down.at[:, columns], dbuf.at[step], d_sem.at[step])

    for step in range(GU_SLOTS):
        for copy in gu_copy(step):
            copy.start()

    barrier = pltpu.get_barrier_semaphore()
    for peer in [index(z_of(k), y, c) for k in (1, 2, 3)] + [y_peer, c_peer]:
        pl.semaphore_signal(barrier, inc=1, device_id=(part, peer), device_id_type=MESH)

    rows = tokens[...].astype(jnp.float32)
    block[me, :, :quarter] = jnp.concatenate(
        [rows[:, q * quarter:(q + 1) * quarter] for q in range(FOLD)], axis=0
    ).astype(jnp.bfloat16)
    block[me, :, quarter:] = jnp.concatenate(
        [by_expert[e] for e in range(EXPERTS)], axis=0).astype(jnp.bfloat16)

    pl.semaphore_wait(barrier, 5)

    def send(source, target, s_sem, r_sem, peer):
        return pltpu.make_async_remote_copy(
            src_ref=source, dst_ref=target, send_sem=s_sem, recv_sem=r_sem,
            device_id=(part, peer), device_id_type=MESH)

    def z_send(k):
        return send(block.at[me], block.at[me], zs.at[k], zr.at[k], index(z_of(k), y, c))

    def y_send(k):
        own = block.at[index(z_of(4 - k), y, c)]
        return send(own, own, ys.at[k], yr.at[k], y_peer)

    def c_send(dy, k):
        own = block.at[index(z_of(4 - k), (y + dy) % 2, c)]
        return send(own, own, cs.at[dy * 4 + k], cr.at[dy * 4 + k], c_peer)

    def assemble(dy, dc):
        base = dc * 32 + dy * 16
        parts = [block[index(z_of(k), (y + dy) % 2, (c + dc) % 2)].astype(jnp.float32)
                 for k in range(4)]
        chosen = jnp.zeros((16, LANES), jnp.float32)
        for q in range(FOLD):
            tile = slice(q // 2 * 8, q // 2 * 8 + 8)
            pairs = [spread(parts[2 * m][tile], parts[2 * m + 1][tile], q % 2) for m in (0, 1)]
            both = jnp.concatenate(pairs, axis=0)
            for h in range(per_quarter):
                x[q * per_quarter + h, base:base + 16, :] = both[
                    :, h * k_rows:(h + 1) * k_rows].astype(jnp.bfloat16)
            chosen = jnp.where(z == q, both[:, quarter:], chosen)
        weight[base:base + 16, :] = chosen

    for k in (2, 3, 1):
        z_send(k).start()
    y_send(0).start()
    c_send(0, 0).start()
    y_send(0).wait_recv()
    c_send(1, 0).start()
    for k in (1, 3, 2):
        z_send(k).wait_recv()
        y_send(k).start()
        c_send(0, k).start()
    for step in range(min(D_EARLY, chunks)):
        d_copy(step).start()
    gate_acc[...] = jnp.zeros_like(gate_acc)
    up_acc[...] = jnp.zeros_like(up_acc)
    assemble(0, 0)
    for k in (1, 3, 2):
        y_send(k).wait_recv()
        c_send(1, k).start()
    assemble(1, 0)
    for k in range(4):
        c_send(0, k).wait_recv()
    assemble(0, 1)
    for k in range(4):
        c_send(1, k).wait_recv()
    assemble(1, 1)

    tile_n = min(512, hid)

    def gate_up(step, carry):
        slot = step % GU_SLOTS
        lhs = x[step]
        for copy, buffer, total in zip(gu_copy(step), (gbuf, ubuf), (gate_acc, up_acc)):
            copy.wait()
            for n in range(hid // tile_n):
                columns = slice(n * tile_n, (n + 1) * tile_n)
                total[:, columns] += jnp.dot(
                    lhs, buffer[slot, :, columns], preferred_element_type=jnp.float32)

        @pl.when(step + GU_SLOTS < K_CHUNKS)
        def _():
            for copy in gu_copy(step + GU_SLOTS):
                copy.start()

        late = -(-(chunks - D_EARLY) // (K_CHUNKS - GU_SLOTS))
        for i in range(max(late, 0)):
            number = D_EARLY + (step - GU_SLOTS) * late + i

            @pl.when((step >= GU_SLOTS) & (number < chunks))
            def _():
                d_copy(number).start()

        return carry

    lax.fori_loop(0, K_CHUNKS, gate_up, 0)
    for n in range(hid // tile_n):
        columns = slice(n * tile_n, (n + 1) * tile_n)
        gate = gate_acc[:, columns]
        hidden[:, columns] = (gate / (1.0 + jnp.exp(-gate)) * up_acc[:, columns]).astype(jnp.bfloat16)

    def a_send(n):
        return send(send_a.at[n], recv_a.at[n], as_.at[n], ar.at[n], c_peer)

    def b_send(n):
        return send(send_b.at[n], recv_b.at[n], bs.at[n], br.at[n], y_peer)

    def t_send(n, k):
        return send(send_c.at[n, k - 1], recv_c.at[n, k - 1], ts.at[n, k - 1], tr.at[n, k - 1],
                    index(z_of(k), y, c))

    def down(step, carry):
        n_d = step - 3 * SKEW

        @pl.when(n_d >= 0)
        def _():
            for k in (1, 2, 3):
                t_send(n_d, k).wait_recv()
            folded[n_d] = keep_c[n_d] + (
                recv_c[n_d, 0].astype(jnp.float32) + recv_c[n_d, 1].astype(jnp.float32)
                + recv_c[n_d, 2].astype(jnp.float32))

        n_c = step - 2 * SKEW

        @pl.when((n_c >= 0) & (n_c < chunks))
        def _():
            b_send(n_c).wait_recv()
            total = keep_b[n_c] + recv_b[n_c].astype(jnp.float32)
            for k in (2, 1, 3, 0):
                half = total[k // 2 * 8:k // 2 * 8 + 8]
                both = jnp.concatenate(
                    [spread(half[:, 2 * m * piece:(2 * m + 1) * piece],
                            half[:, (2 * m + 1) * piece:(2 * m + 2) * piece], k % 2)
                     for m in (0, 1)], axis=0)
                if k == 0:
                    keep_c[n_c] = both
                else:
                    send_c[n_c, k - 1] = both.astype(jnp.bfloat16)
                    t_send(n_c, k).start()

        n_b = step - SKEW

        @pl.when((n_b >= 0) & (n_b < chunks))
        def _():
            a_send(n_b).wait_recv()
            send_b[n_b] = (keep_a[n_b, 16:, :] + recv_a[n_b, 16:, :].astype(jnp.float32)).astype(jnp.bfloat16)
            b_send(n_b).start()
            keep_b[n_b] = keep_a[n_b, :16, :] + recv_a[n_b, :16, :].astype(jnp.float32)

        @pl.when(step < chunks)
        def _():
            d_copy(step).wait()
            scale = weight[...]
            product = jnp.dot(hidden[...], dbuf[step], preferred_element_type=jnp.float32)
            product = product * jnp.concatenate([scale] * (CHUNK // LANES), axis=1)
            send_a[step] = product[32:].astype(jnp.bfloat16)
            a_send(step).start()
            keep_a[step] = product[:32]

        return carry

    lax.fori_loop(0, chunks + 3 * SKEW, down, 0)

    for n in range(chunks):
        pieces = []
        for j in range(FOLD):
            half = folded[n, j // 2 * 8:j // 2 * 8 + 8, :]
            pieces.append(pltpu.roll(half, 4, 0) if j % 2 else half)
        whole = jnp.concatenate(pieces, axis=1)
        out[:, n * CHUNK:(n + 1) * CHUNK] = whole[:ROWS_DEV].astype(jnp.bfloat16)

    for k in (1, 2, 3):
        z_send(k).wait_send()
    for k in range(4):
        y_send(k).wait_send()
        c_send(0, k).wait_send()
        c_send(1, k).wait_send()

    def drain(n, carry):
        a_send(n).wait_send()
        b_send(n).wait_send()
        for k in (1, 2, 3):
            t_send(n, k).wait_send()
        return carry

    lax.fori_loop(0, chunks, drain, 0)


def fused(tokens, route_ids, gate_values, w_gate, w_up, w_down):
    width = tokens.shape[1]
    hid = w_gate.shape[1]
    chunks = width // CHUNK
    quarter = width // FOLD
    k_rows = width // K_CHUNKS
    piece = CHUNK // FOLD
    rows = DEVICES * ROWS_DEV
    bf16, f32, dma = jnp.bfloat16, jnp.float32, pltpu.SemaphoreType.DMA
    scratch = [
        pltpu.VMEM((DEVICES, 16, quarter + LANES), bf16),
        pltpu.VMEM((K_CHUNKS, rows, k_rows), bf16),
        pltpu.VMEM((rows, LANES), f32),
        pltpu.VMEM((GU_SLOTS, k_rows, hid), bf16),
        pltpu.VMEM((GU_SLOTS, k_rows, hid), bf16),
        pltpu.VMEM((chunks, hid, CHUNK), bf16),
        pltpu.VMEM((rows, hid), f32),
        pltpu.VMEM((rows, hid), f32),
        pltpu.VMEM((rows, hid), bf16),
        pltpu.VMEM((chunks, 32, CHUNK), bf16),
        pltpu.VMEM((chunks, 32, CHUNK), bf16),
        pltpu.VMEM((chunks, 32, CHUNK), f32),
        pltpu.VMEM((chunks, 16, CHUNK), bf16),
        pltpu.VMEM((chunks, 16, CHUNK), bf16),
        pltpu.VMEM((chunks, 16, CHUNK), f32),
        pltpu.VMEM((chunks, 3, 16, piece), bf16),
        pltpu.VMEM((chunks, 3, 16, piece), bf16),
        pltpu.VMEM((chunks, 16, piece), f32),
        pltpu.VMEM((chunks, 16, piece), f32),
        dma((GU_SLOTS,)), dma((GU_SLOTS,)), dma((chunks,)),
        dma((4,)), dma((4,)), dma((4,)), dma((4,)), dma((8,)), dma((8,)),
        dma((chunks,)), dma((chunks,)), dma((chunks,)), dma((chunks,)),
        dma((chunks, 3)), dma((chunks, 3)),
    ]
    chosen = route_ids[None, :, :] == jnp.arange(EXPERTS, dtype=jnp.int32)[:, None, None]
    by_expert = jnp.sum(jnp.where(chosen, gate_values.astype(f32)[None], 0.0), axis=2)
    by_expert = jnp.broadcast_to(by_expert[:, :, None], (EXPERTS, ROWS_DEV, LANES))
    vmem = pl.BlockSpec(memory_space=pltpu.VMEM)
    hbm = pl.BlockSpec(memory_space=pl.ANY)
    return pl.pallas_call(
        functools.partial(kernel, (width, hid, chunks)),
        out_shape=jax.ShapeDtypeStruct((ROWS_DEV, width), bf16),
        in_specs=[vmem, vmem, hbm, hbm, hbm],
        out_specs=vmem,
        scratch_shapes=scratch,
        compiler_params=pltpu.CompilerParams(
            collective_id=0, has_side_effects=True, vmem_limit_bytes=60 * 2**20),
        cost_estimate=pl.CostEstimate(
            flops=6 * rows * width * hid, bytes_accessed=6 * width * hid, transcendentals=rows * hid),
    )(tokens, by_expert, w_gate, w_up, w_down)


def partner(shard, axis, stride):
    return lax.ppermute(shard, axis, [(i, i ^ 1 << stride) for i in range(lax.axis_size(axis))])


def from_behind(block, axis, distance):
    devices = range(lax.axis_size(axis))
    route = [((i - distance) % len(devices), i) for i in devices]
    return lax.ppermute(block, axis, route)


def expert_blocks(compact, occupied, w_gate, w_up, w_down):
    capacity = compact.shape[0]

    def block_step(block_index, buffer):

        def block_work(inner):
            block_rows = lax.dynamic_slice_in_dim(compact, block_index * BLOCK, BLOCK, 0)
            gate_proj = jnp.dot(block_rows, w_gate, preferred_element_type=jnp.float32)
            up_proj = jnp.dot(block_rows, w_up, preferred_element_type=jnp.float32)
            hidden = (jax.nn.silu(gate_proj) * up_proj).astype(jnp.bfloat16)
            output_rows = jnp.dot(hidden, w_down, preferred_element_type=jnp.float32)
            return lax.dynamic_update_slice_in_dim(inner, output_rows, block_index * BLOCK, 0)

        def block_skip(inner):
            return inner

        return lax.cond(block_index * BLOCK < occupied, block_work, block_skip, buffer)

    start_buffer = jnp.zeros((capacity, w_down.shape[1]), jnp.float32)
    return lax.fori_loop(0, capacity // BLOCK, block_step, start_buffer)


def per_device(tokens, route_ids, gate_values, w_gate, w_up, w_down):
    tensor_size = lax.axis_size("tensor")
    group_size = tensor_size // EXPERTS
    my_index = lax.axis_index("tensor")
    expert = my_index // group_size
    local_rows = tokens.shape[0]
    width = tokens.shape[1]
    total_rows = local_rows * tensor_size
    capacity = (total_rows + BLOCK - 1) // BLOCK * BLOCK
    all_routes = lax.all_gather(route_ids, "tensor", axis=0, tiled=True)
    routed = all_routes == expert
    selected = jnp.any(routed, axis=1).astype(jnp.int32)
    occupied = jnp.sum(selected)
    expert_list = jnp.arange(EXPERTS, dtype=jnp.int32)
    local_hits = jnp.any(route_ids[:, :, None] == expert_list[None, None, :], axis=1).astype(
        jnp.int32
    )
    local_place = jnp.cumsum(local_hits, axis=0) - 1
    target = jnp.where(local_hits > 0, local_place, MOST)
    row_numbers = jnp.broadcast_to(jnp.arange(local_rows, dtype=jnp.int32)[:, None], target.shape)
    send_rows = (
        jnp.full((EXPERTS, MOST), local_rows, jnp.int32)
        .at[jnp.broadcast_to(expert_list[None, :], target.shape), target]
        .set(row_numbers, mode="drop")
    )
    outgoing = jnp.take(tokens, send_rows.reshape(-1), axis=0, mode="fill", fill_value=0)
    outgoing = outgoing.reshape(EXPERTS, 1, MOST, width)
    outgoing = jnp.broadcast_to(outgoing, (EXPERTS, group_size, MOST, width)).reshape(
        tensor_size * MOST, width
    )
    received = lax.all_to_all(outgoing, "tensor", split_axis=0, concat_axis=0, tiled=True)
    per_source = jnp.sum(selected.reshape(tensor_size, local_rows), axis=1)
    source_start = jnp.cumsum(per_source) - per_source
    place = jnp.arange(MOST, dtype=jnp.int32)
    landing = jnp.where(
        place[None, :] < per_source[:, None], source_start[:, None] + place[None, :], capacity
    )
    inverse = (
        jnp.full((capacity,), tensor_size * MOST, jnp.int32)
        .at[landing.reshape(-1)]
        .set(jnp.arange(tensor_size * MOST, dtype=jnp.int32), mode="drop")
    )
    compact = jnp.take(received, inverse, axis=0, mode="fill", fill_value=0)
    partial_value = expert_blocks(compact, occupied, w_gate, w_up, w_down)
    returning = jnp.take(partial_value, landing.reshape(-1), axis=0, mode="fill", fill_value=0)
    levels = group_size.bit_length() - 1
    buffer = jnp.transpose(returning.reshape(EXPERTS, group_size, MOST, width), (1, 0, 2, 3))
    for bit in range(levels - 1, -1, -1):
        half = buffer.shape[0] // 2
        lower = buffer[:half]
        upper = buffer[half:]
        high_side = my_index >> bit & 1 == 1
        keep = jnp.where(high_side, upper, lower)
        give = jnp.where(high_side, lower, upper)
        buffer = keep + partner(give, "tensor", bit)
    reduced = buffer[0]
    collected = jnp.zeros((EXPERTS, MOST, width), jnp.float32)
    own_piece = lax.dynamic_index_in_dim(reduced, expert, 0, keepdims=True)
    collected = lax.dynamic_update_slice_in_dim(collected, own_piece, expert, 0)
    for offset in range(1, EXPERTS):
        piece = lax.dynamic_index_in_dim(reduced, (expert + offset) % EXPERTS, 0, keepdims=True)
        arrived_piece = from_behind(piece, "tensor", offset * group_size)
        source_expert = (expert - offset + EXPERTS) % EXPERTS
        collected = lax.dynamic_update_slice_in_dim(collected, arrived_piece, source_expert, 0)
    per_expert = collected.reshape(EXPERTS * MOST, width)
    mixed_rows = jnp.zeros((local_rows, width), jnp.float32)
    for column in range(2):
        chosen = route_ids[:, column]
        chosen_place = jnp.take_along_axis(local_place, chosen[:, None], axis=1)[:, 0]
        picked = jnp.take(per_expert, chosen * MOST + chosen_place, axis=0)
        mixed_rows = mixed_rows + gate_values[:, column].astype(jnp.float32)[:, None] * picked
    return mixed_rows.astype(jnp.bfloat16)


def solution(mesh):
    in_specs = (
        P(("parts", "tensor"), None),
        P(("parts", "tensor"), None),
        P(("parts", "tensor"), None),
        P(None, "tensor"),
        P(None, "tensor"),
        P("tensor", None),
    )
    out_specs = P(("parts", "tensor"), None)
    rows = ROWS_DEV * DEVICES

    def whole(tokens, route_ids, gate_values, w_gate, w_up, w_down):
        width, hid = w_gate.shape[0], w_gate.shape[1] // mesh.shape["tensor"]
        fits = mesh.shape["tensor"] == DEVICES and tokens.shape[0] == rows * mesh.shape["parts"]
        fits = fits and width % (K_CHUNKS * LANES) == 0 and hid % 512 == 0
        fits = fits and width * hid <= 6144 * 2048
        return shard(fused if fits else per_device)(
            tokens, route_ids, gate_values, w_gate, w_up, w_down)

    shard = lambda body: jax.shard_map(
        body, mesh=mesh, in_specs=in_specs, out_specs=out_specs, check_vma=False
    )
    return whole
```
